512 devices in a mesh: outer: 32 (over y, z_lo, core), inner: 16 (over x, z_hi).
Axes of the slice: x: 4, y: 4, z: 16 (z_hi: 4, z_lo: 4; z = z_hi * 4 + z_lo), core: 2. Of those that a mesh axis runs over, the one named last changes fastest.
Arguments:
- queries: bfloat16 [49152, 2560], P(('outer', 'inner')), may hold values from -120 to 120
- keys: bfloat16 [49152, 2560], P(('outer', 'inner')), may hold values from -4 to 4
- values: bfloat16 [49152, 2560], P(('outer', 'inner')), may hold values from -6 to 6
- doc_start: int32 [49152], P(('outer', 'inner')), may hold values from 0 to 49151, as said below
Outputs:
- attended: bfloat16 [49152, 2560], P(('outer', 'inner'))
The draws below stay inside these ranges and needn't reach their ends.
Inputs may be any that keep to these rules, and one draw needn't show every extreme that they name: doc_start[p] is the first position of the document that holds p: never decreasing, doc_start[p] <= p, p - doc_start[p] < 480; the first document has exactly (5) * 96 positions.
All inputs are finite; a program needn't handle non-finite values.
Results may differ from the reference program's by a relative error of at most 0.0044.
Values may be sent and summed in bfloat16 or wider, within the bound.
A program may use at most 64 MiB of HBM per device.

```python
import math
import jax
import jax.numpy as jnp
from jax import lax

HEADS = 20
HD = 128
TOK_DEV = 96
SPAN = 6
TOKENS = 49152


def base_pair(key):
    query_key, key_key = jax.random.split(key, 2)
    shape = (TOKENS, HEADS * HD)
    query_base = jnp.clip(jax.random.normal(query_key, shape, jnp.float32), -4.0, 4.0)
    key_base = jnp.clip(jax.random.normal(key_key, shape, jnp.float32), -4.0, 4.0)
    return (query_base, key_base)


def draw_queries(key, part):
    query_base, key_base = base_pair(key)
    result = query_base
    return result.astype(jnp.bfloat16)


def draw_keys(key, part):
    query_base, key_base = base_pair(key)
    result = key_base
    return result.astype(jnp.bfloat16)


def draw_doc_start(key, part):
    key = jax.random.fold_in(key, 11)
    longest = (SPAN - 1) * TOK_DEV
    kind_key, long_key, short_key = jax.random.split(key, 3)
    is_long = jax.random.randint(kind_key, (TOKENS,), 0, 3) == 0
    long_len = jax.random.randint(long_key, (TOKENS,), longest // 2, longest + 1)
    short_len = jax.random.randint(short_key, (TOKENS,), 1, TOK_DEV // 2 + 1)
    lengths = jnp.where(is_long, long_len, short_len).astype(jnp.int32)
    lengths = lengths.at[0].set(longest)
    starts = jnp.concatenate([jnp.zeros((1,), jnp.int32), jnp.cumsum(lengths)[:-1].astype(jnp.int32)])
    position = jnp.arange(TOKENS, dtype=jnp.int32)
    which = jnp.searchsorted(starts, position, side='right').astype(jnp.int32) - 1
    return starts[which].astype(jnp.int32)


def shard_levels(rng, extent, cuts, least, high):
    loudness = 1.0
    for axis_at, parts in cuts:
        draws = jax.random.uniform(jax.random.fold_in(jax.random.fold_in(rng, 6), axis_at), (parts,), jnp.float32, least / len(cuts), high / len(cuts))
        loudness = loudness * jnp.repeat(jnp.exp(draws), extent[axis_at] // parts).reshape((-1,) + (1,) * (len(extent) - 1 - axis_at))
    return loudness


def noise(rng, dims, spread, bound, cuts=(), held_as=jnp.bfloat16):
    array = spread * jax.random.normal(rng, dims, jnp.float32)
    if cuts:
        array = array * shard_levels(rng, dims, cuts, -0.22, 0.18)
    return jnp.clip(array, -bound, bound).astype(held_as)


def setup_inputs(seed: int = 0) -> dict:
    key_list = jax.random.split(jax.random.key(seed), 5)
    return {
        "queries": draw_queries(jax.random.fold_in(key_list[4], 71), 0),
        "keys": draw_keys(jax.random.fold_in(key_list[4], 71), 0),
        "values": noise(key_list[2], (TOKENS, HEADS * HD), 1.0, 6.0, ((0, 512),)),
        "doc_start": draw_doc_start(jax.random.fold_in(key_list[4], 71), 0),
    }


def attend(query_rows, key_rows, value_rows, query_pos, key_pos, starts):
    count = query_rows.shape[0]
    width = query_rows.shape[1]
    heads = width // HD
    query_heads = query_rows.astype(jnp.float32).reshape(count, heads, HD)
    key_heads = key_rows.astype(jnp.float32).reshape(-1, heads, HD)
    value_heads = value_rows.astype(jnp.float32).reshape(-1, heads, HD)
    scores = jnp.einsum('qhd,khd->hqk', query_heads, key_heads) * (1.0 / math.sqrt(HD))
    allowed = (key_pos[None, :] >= starts[:, None]) & (key_pos[None, :] <= query_pos[:, None])
    scores = jnp.where(allowed[None], scores, -jnp.inf)
    largest = lax.optimization_barrier(jnp.max(scores, axis=-1, keepdims=True))
    expsum = jnp.exp(scores - largest)
    total = lax.optimization_barrier(jnp.sum(expsum, axis=-1, keepdims=True))
    weights = (expsum / total).astype(jnp.bfloat16)
    mixed = jnp.einsum('hqk,khd->qhd', weights.astype(jnp.float32), value_heads)
    return mixed.reshape(count, width).astype(jnp.bfloat16)

def reference(queries, keys, values, doc_start):
    width = HEADS * HD
    margin = (SPAN - 1) * TOK_DEV
    padded_keys = jnp.concatenate([jnp.zeros((margin, width), jnp.bfloat16), keys], axis=0)
    padded_values = jnp.concatenate([jnp.zeros((margin, width), jnp.bfloat16), values], axis=0)
    blocks = TOKENS // TOK_DEV

    def one_block(index):
        first = (index * TOK_DEV).astype(jnp.int32)
        query_rows = lax.dynamic_slice_in_dim(queries, first, TOK_DEV, 0)
        starts = lax.dynamic_slice_in_dim(doc_start, first, TOK_DEV, 0)
        key_rows = lax.dynamic_slice_in_dim(padded_keys, first, SPAN * TOK_DEV, 0)
        value_rows = lax.dynamic_slice_in_dim(padded_values, first, SPAN * TOK_DEV, 0)
        query_pos = first + jnp.arange(TOK_DEV, dtype=jnp.int32)
        key_pos = first - margin + jnp.arange(SPAN * TOK_DEV, dtype=jnp.int32)
        return attend(query_rows, key_rows, value_rows, query_pos, key_pos, starts)
    result = lax.map(one_block, jnp.arange(blocks, dtype=jnp.int32))
    return result.reshape(TOKENS, width)
```

```python
import functools
import math

import jax
import jax.numpy as jnp
from jax import lax
from jax.experimental import pallas as pl
from jax.experimental.pallas import tpu as pltpu
from jax.sharding import PartitionSpec as P

HD = 128
HEADS = 20
TOK = 96
SPAN = 6
COLS = 4
GROUP = HEADS // COLS
ROW = COLS * TOK
BACK = (SPAN - 1) * TOK
KEYS = BACK + ROW
TILE = 128
WIN = TILE + BACK
SHIFTS = (2, 1, 3)
MESH = pl.DeviceIdType.MESH


def wrap(a, n):
    return lax.rem(a + n, n)


def next_row(o, x, c):
    last = x // 3
    turn = last * (lax.rem(o, 8) // 7)
    return lax.rem(o + last, 32), lax.rem(x + 1, 4), lax.rem(c + turn, COLS)


def prev_row(o, x, c):
    first = (3 - x) // 3
    turn = first * ((7 - lax.rem(o, 8)) // 7)
    return wrap(o - first, 32), wrap(x - 1, 4), wrap(c - turn, COLS)


def device(o, x, c):
    return (o, x * 4 + c)


def kernel(q_ref, k_ref, v_ref, start_ref, out_ref, kv, qb, ob, sb, sc, bias,
           kv_send, kv_recv, q_send, q_recv, o_send, o_recv, x_send, x_recv, s_send, s_recv,
           local):
    o = lax.axis_index("outer")
    inner = lax.axis_index("inner")
    x, c = inner // 4, lax.rem(inner, 4)
    y = o // 8
    mine = wrap(c - y, COLS)
    n1 = next_row(o, x, c)
    n2 = next_row(*n1)
    p1 = prev_row(o, x, c)
    p2 = prev_row(*p1)
    peers = [device(o, x, lax.rem(c + s, COLS)) for s in SHIFTS]
    groups = [lax.rem(mine + s, COLS) for s in SHIFTS]

    barrier = pltpu.get_barrier_semaphore()
    for who in peers + [device(*p1), device(*p2)]:
        pl.semaphore_signal(barrier, inc=1, device_id=who, device_id_type=MESH)

    rows = pl.ds(pl.multiple_of(c * TOK, TOK), TOK)
    own = pl.ds(pl.multiple_of(BACK + c * TOK, TOK), TOK)

    def lanes(group, i):
        return pl.ds(pl.multiple_of(group * (GROUP * HD) + i * HD, HD), HD)

    def local_copies(i):
        return [
            pltpu.make_async_copy(k_ref.at[:, lanes(mine, i)], kv.at[i, 0, own], local.at[0, i]),
            pltpu.make_async_copy(v_ref.at[:, lanes(mine, i)], kv.at[i, 1, own], local.at[1, i]),
            pltpu.make_async_copy(q_ref.at[:, lanes(mine, i)], qb.at[i, rows], local.at[2, i]),
        ]

    def start_copies():
        return [pltpu.make_async_remote_copy(
            src_ref=start_ref, dst_ref=sb.at[c], send_sem=s_send.at[n], recv_sem=s_recv.at[n],
            device_id=peers[n], device_id_type=MESH) for n in range(3)]

    def kv_copies(i):
        return [pltpu.make_async_remote_copy(
            src_ref=ref.at[:, lanes(groups[n], i)], dst_ref=kv.at[i, t, own],
            send_sem=kv_send.at[t, i, n], recv_sem=kv_recv.at[t, i, n],
            device_id=peers[n], device_id_type=MESH)
            for t, ref in enumerate((k_ref, v_ref)) for n in range(3)]

    def q_copies(i):
        return [pltpu.make_async_remote_copy(
            src_ref=q_ref.at[:, lanes(groups[n], i)], dst_ref=qb.at[i, rows],
            send_sem=q_send.at[i, n], recv_sem=q_recv.at[i, n],
            device_id=peers[n], device_id_type=MESH) for n in range(3)]

    def x_copies(i):
        return [
            pltpu.make_async_remote_copy(
                src_ref=kv.at[i, :, pl.ds(BACK, ROW)], dst_ref=kv.at[i, :, pl.ds(TOK, ROW)],
                send_sem=x_send.at[0, i], recv_sem=x_recv.at[0, i],
                device_id=device(*n1), device_id_type=MESH),
            pltpu.make_async_remote_copy(
                src_ref=kv.at[i, :, pl.ds(KEYS - TOK, TOK)], dst_ref=kv.at[i, :, pl.ds(0, TOK)],
                send_sem=x_send.at[1, i], recv_sem=x_recv.at[1, i],
                device_id=device(*n2), device_id_type=MESH),
        ]

    def o_copies(i):
        return [pltpu.make_async_remote_copy(
            src_ref=ob.at[i, pl.ds(pl.multiple_of(lax.rem(c + s, COLS) * TOK, TOK), TOK)],
            dst_ref=out_ref.at[:, lanes(mine, i)],
            send_sem=o_send.at[i, n], recv_sem=o_recv.at[i, n],
            device_id=peers[n], device_id_type=MESH) for n, s in enumerate(SHIFTS)]

    def o_local(i):
        return pltpu.make_async_copy(ob.at[i, rows], out_ref.at[:, lanes(mine, i)], local.at[3, i])

    own_start = pltpu.make_async_copy(start_ref, sb.at[c], local.at[4, 0])
    own_start.start()
    for i in range(GROUP):
        for copy in local_copies(i):
            copy.start()

    pl.semaphore_wait(barrier, 5)
    for copy in start_copies():
        copy.start()
    for i in range(GROUP):
        for copy in kv_copies(i):
            copy.start()
    for i in range(GROUP):
        for copy in q_copies(i):
            copy.start()

    own_start.wait()
    for copy in start_copies():
        copy.wait()
    for b in range(COLS):
        spread = jnp.broadcast_to(sb[b, 0:1, :], (HD, HD)).T
        sc[b * TOK:(b + 1) * TOK, :] = spread[:TOK, :]
    row = o * 4 + x
    for t in range(ROW // TILE):
        first = row * ROW + t * TILE
        key_pos = first - BACK + lax.broadcasted_iota(jnp.int32, (TILE, WIN), 1)
        query_pos = first + lax.broadcasted_iota(jnp.int32, (TILE, WIN), 0)
        starts = sc[t * TILE:(t + 1) * TILE, 0:1]
        allowed = (key_pos >= starts) & (key_pos <= query_pos)
        bias[t] = jnp.where(allowed, 0.0, -jnp.inf)

    @pl.loop(0, GROUP)
    def _(i):
        for copy in local_copies(i)[:2]:
            copy.wait()
        for copy in kv_copies(i):
            copy.wait_recv()
        for copy in x_copies(i):
            copy.start()

    @pl.loop(0, GROUP)
    def _(i):
        local_copies(i)[2].wait()
        for copy in q_copies(i):
            copy.wait_recv()
        for copy in x_copies(i):
            copy.wait_recv()
        for t in range(ROW // TILE):
            low = t * TILE
            scores = lax.dot_general(
                qb[i, low:low + TILE, :], kv[i, 0, low:low + WIN, :],
                (((1,), (1,)), ((), ())), preferred_element_type=jnp.float32)
            scores = scores * (1.0 / math.sqrt(HD)) + bias[t]
            largest = jnp.max(scores, axis=-1, keepdims=True)
            expsum = jnp.exp(scores - largest)
            total = jnp.sum(expsum, axis=-1, keepdims=True)
            weights = (expsum * (1.0 / total)).astype(jnp.bfloat16)
            mixed = jnp.dot(weights, kv[i, 1, low:low + WIN, :], preferred_element_type=jnp.float32)
            ob[i, low:low + TILE, :] = mixed.astype(jnp.bfloat16)
        o_local(i).start()
        for copy in o_copies(i):
            copy.start()

    @pl.loop(0, GROUP)
    def _(i):
        for copy in kv_copies(i) + q_copies(i) + x_copies(i):
            copy.wait_send()
        o_local(i).wait()
        for copy in o_copies(i):
            copy.wait()


def body(queries, keys, values, doc_start):
    starts = jnp.pad(doc_start[None, :], ((0, 7), (0, HD - TOK)))
    width = HEADS * HD
    dma = pltpu.SemaphoreType.DMA
    hbm = pl.BlockSpec(memory_space=pltpu.HBM)
    return pl.pallas_call(
        kernel,
        out_shape=jax.ShapeDtypeStruct((TOK, width), jnp.bfloat16),
        in_specs=[hbm, hbm, hbm, hbm],
        out_specs=hbm,
        scratch_shapes=[
            pltpu.VMEM((GROUP, 2, KEYS, HD), jnp.bfloat16),
            pltpu.VMEM((GROUP, ROW, HD), jnp.bfloat16),
            pltpu.VMEM((GROUP, ROW, HD), jnp.bfloat16),
            pltpu.VMEM((COLS, 8, HD), jnp.int32),
            pltpu.VMEM((ROW, HD), jnp.int32),
            pltpu.VMEM((ROW // TILE, TILE, WIN), jnp.float32),
            dma((2, GROUP, 3)), dma((2, GROUP, 3)),
            dma((GROUP, 3)), dma((GROUP, 3)),
            dma((GROUP, 3)), dma((GROUP, 3)),
            dma((2, GROUP)), dma((2, GROUP)),
            dma((3,)), dma((3,)),
            dma((5, GROUP)),
        ],
        compiler_params=pltpu.CompilerParams(
            collective_id=0, has_side_effects=True, vmem_limit_bytes=32 * 1024 * 1024),
        cost_estimate=pl.CostEstimate(
            flops=4 * TOK * SPAN * TOK * width, bytes_accessed=8 * TOK * width,
            transcendentals=TOK * SPAN * TOK * HEADS),
    )(queries, keys, values, starts)


def solution(mesh):
    rows = P(("outer", "inner"), None)
    return jax.shard_map(
        body,
        mesh=mesh,
        in_specs=(rows, rows, rows, P(("outer", "inner"))),
        out_specs=rows,
        check_vma=False,
    )
```

```python
import functools
import math

import jax
import jax.numpy as jnp
from jax import lax
from jax.experimental import pallas as pl
from jax.experimental.pallas import tpu as pltpu
from jax.sharding import PartitionSpec as P

HD = 128
HEADS = 20
TOK = 96
SPAN = 6
COLS = 4
GROUP = HEADS // COLS
ROW = COLS * TOK
BACK = (SPAN - 1) * TOK
KEYS = BACK + ROW
TILE = 128
WIN = TILE + BACK
MESH = pl.DeviceIdType.MESH
BF16 = jnp.bfloat16


def wrap(a, n):
    return lax.rem(a + n, n)


def device(x, y, z, core):
    return ((y * 4 + lax.rem(z, 4)) * 2 + core, x * 4 + z // 4)


def row_device(x, y, z, core, by, shift):
    r = core * 4 + x + by + 8
    carry = r // 8 - 1
    r = lax.rem(r, 8)
    z2 = wrap(z + shift, 16)
    at = z2 if by > 0 else z
    y2 = wrap(y + carry * ((3 - lax.rem(at, 4)) // 3), 4)
    return device(lax.rem(r, 4), y2, z2, r // 4)


def kernel(q_ref, k_ref, v_ref, start_ref, out_ref, kv, qb, ob, sb, sc, bias,
           kv_send, kv_recv, q_send, q_recv, o_send, o_recv, x_send, x_recv, s_send, s_recv):
    o = lax.axis_index("outer")
    inner = lax.axis_index("inner")
    x, zh = inner // 4, lax.rem(inner, 4)
    core, zl, y = lax.rem(o, 2), lax.rem(o // 2, 4), o // 8
    z = zh * 4 + zl
    r = core * 4 + x

    def ahead(i):
        return (r + i) // 8

    def along(dz):
        return device(x, y, wrap(z + dz, 16), core)

    def column(i):
        return wrap(z - ahead(i), 16) // 4

    def group(i):
        return wrap(column(i) - y, 4)

    barrier = pltpu.get_barrier_semaphore()
    greeted = [along(-4 * n) for n in (1, 2, 3)]
    greeted += [along(-1 - 4 * n) for n in range(4)] + [along(1 + 4 * n - 16) for n in range(4)]
    greeted += [row_device(x, y, z, core, -by, -shift) for by in (1, 2) for shift in (0, 1)]
    for who in greeted:
        pl.semaphore_signal(barrier, inc=1, device_id=who, device_id_type=MESH)

    rows = pl.ds(pl.multiple_of(zh * TOK, TOK), TOK)
    own = pl.ds(pl.multiple_of(BACK + zh * TOK, TOK), TOK)

    def lanes(g, i):
        return pl.ds(pl.multiple_of(g * (GROUP * HD) + i * HD, HD), HD)

    class Copy:
        def __init__(self, src, dst, send, recv, dz, here):
            self.away = pltpu.make_async_remote_copy(
                src_ref=src, dst_ref=dst, send_sem=send, recv_sem=recv,
                device_id=along(dz), device_id_type=MESH)
            self.home = None if here is None else pltpu.make_async_copy(src, dst, recv)
            self.here = here

        def do(self, away, home):
            if self.here is None:
                away(self.away)
                return
            pl.when(self.here == 0)(lambda: home(self.home))
            pl.when(self.here != 0)(lambda: away(self.away))

        def start(self):
            self.do(lambda c: c.start(), lambda c: c.start())

        def wait_recv(self):
            self.do(lambda c: c.wait_recv(), lambda c: c.wait())

        def wait_send(self):
            self.do(lambda c: c.wait_send(), lambda c: None)

    ORDER = (2, 1, 3, 0)

    def out_lanes(i, n):
        return lanes(wrap(zh + n - y, 4), i)

    def kv_copies(i):
        s = ahead(i)
        return [Copy(ref.at[:, out_lanes(i, n)], kv.at[i, t, own], kv_send.at[t, i, n], kv_recv.at[t, i, n],
                     4 * n + s, s if n == 0 else None)
                for t, ref in enumerate((k_ref, v_ref)) for n in ORDER]

    def q_copies(i):
        s = ahead(i)
        return [Copy(q_ref.at[:, out_lanes(i, n)], qb.at[i, rows], q_send.at[i, n], q_recv.at[i, n],
                     4 * n + s, s if n == 0 else None) for n in ORDER]

    def start_copies():
        return [Copy(start_ref, sb.at[s, zh], s_send.at[s, n], s_recv.at[s, n], 4 * n + s,
                     jnp.int32(0) if n + s == 0 else None) for s in range(2) for n in range(4)]

    def o_copies(i):
        s = ahead(i)
        return [Copy(ob.at[i, pl.ds(pl.multiple_of(wrap(column(i) - n, COLS) * TOK, TOK), TOK)],
                     out_ref.at[:, lanes(group(i), i)], o_send.at[i, n], o_recv.at[i, n],
                     -4 * n - s, s if n == 0 else None) for n in ORDER]

    def x_copies(i):
        copies = []
        for by, src, dst in ((1, pl.ds(BACK, ROW), pl.ds(TOK, ROW)), (2, pl.ds(KEYS - TOK, TOK), pl.ds(0, TOK))):
            there = r + by
            shift = there // 8 + (lax.rem(there, 8) + i) // 8 - ahead(i)
            copies.append(pltpu.make_async_remote_copy(
                src_ref=kv.at[i, :, src], dst_ref=kv.at[i, :, dst],
                send_sem=x_send.at[by - 1, i], recv_sem=x_recv.at[by - 1, i],
                device_id=row_device(x, y, z, core, by, shift), device_id_type=MESH))
        return copies

    pl.semaphore_wait(barrier, len(greeted))
    for copy in start_copies():
        copy.start()
    for i in range(GROUP):
        for copy in kv_copies(i):
            copy.start()
    for i in range(GROUP):
        for copy in q_copies(i):
            copy.start()

    for copy in start_copies():
        copy.wait_recv()
    for s in range(2):
        for b in range(COLS):
            spread = jnp.broadcast_to(sb[s, b, 0:1, :], (HD, HD)).T
            sc[b * TOK:(b + 1) * TOK, :] = spread[:TOK, :]
        row = ((y * 4 + lax.rem(wrap(z - s, 16), 4)) * 2 + core) * 4 + x
        for t in range(ROW // TILE):
            first = row * ROW + t * TILE
            key_pos = first - BACK + lax.broadcasted_iota(jnp.int32, (TILE, WIN), 1)
            query_pos = first + lax.broadcasted_iota(jnp.int32, (TILE, WIN), 0)
            starts = sc[t * TILE:(t + 1) * TILE, 0:1]
            allowed = (key_pos >= starts) & (key_pos <= query_pos)
            bias[s, t] = jnp.where(allowed, 0.0, -jnp.inf)

    @pl.loop(0, GROUP)
    def _(i):
        for copy in kv_copies(i):
            copy.wait_recv()
        for copy in x_copies(i):
            copy.start()

    @pl.loop(0, GROUP)
    def _(i):
        for copy in q_copies(i):
            copy.wait_recv()
        for copy in x_copies(i):
            copy.wait_recv()
        for t in range(ROW // TILE):
            low = t * TILE
            scores = lax.dot_general(
                qb[i, low:low + TILE, :], kv[i, 0, low:low + WIN, :],
                (((1,), (1,)), ((), ())), preferred_element_type=jnp.float32)
            scores = scores * (1.0 / math.sqrt(HD)) + bias[ahead(i), t]
            largest = jnp.max(scores, axis=-1, keepdims=True)
            expsum = jnp.exp(scores - largest)
            total = jnp.sum(expsum, axis=-1, keepdims=True)
            weights = (expsum * (1.0 / total)).astype(BF16)
            mixed = jnp.dot(weights, kv[i, 1, low:low + WIN, :], preferred_element_type=jnp.float32)
            ob[i, low:low + TILE, :] = mixed.astype(BF16)
        for copy in o_copies(i):
            copy.start()

    for copy in start_copies():
        copy.wait_send()

    @pl.loop(0, GROUP)
    def _(i):
        for copy in kv_copies(i) + q_copies(i) + x_copies(i):
            copy.wait_send()
        for copy in o_copies(i):
            copy.wait_recv()
            copy.wait_send()


def body(queries, keys, values, doc_start):
    starts = jnp.pad(doc_start[None, :], ((0, 7), (0, HD - TOK)))
    width = HEADS * HD
    dma = pltpu.SemaphoreType.DMA
    hbm = pl.BlockSpec(memory_space=pltpu.HBM)
    return pl.pallas_call(
        kernel,
        out_shape=jax.ShapeDtypeStruct((TOK, width), jnp.bfloat16),
        in_specs=[hbm, hbm, hbm, hbm],
        out_specs=hbm,
        scratch_shapes=[
            pltpu.VMEM((GROUP, 2, KEYS, HD), jnp.bfloat16),
            pltpu.VMEM((GROUP, ROW, HD), jnp.bfloat16),
            pltpu.VMEM((GROUP, ROW, HD), jnp.bfloat16),
            pltpu.VMEM((2, COLS, 8, HD), jnp.int32),
            pltpu.VMEM((ROW, HD), jnp.int32),
            pltpu.VMEM((2, ROW // TILE, TILE, WIN), jnp.float32),
            dma((2, GROUP, COLS)), dma((2, GROUP, COLS)),
            dma((GROUP, COLS)), dma((GROUP, COLS)),
            dma((GROUP, COLS)), dma((GROUP, COLS)),
            dma((2, GROUP)), dma((2, GROUP)),
            dma((2, COLS)), dma((2, COLS)),
        ],
        compiler_params=pltpu.CompilerParams(
            collective_id=0, has_side_effects=True, vmem_limit_bytes=32 * 1024 * 1024),
        cost_estimate=pl.CostEstimate(
            flops=4 * TOK * SPAN * TOK * width, bytes_accessed=8 * TOK * width,
            transcendentals=TOK * SPAN * TOK * HEADS),
    )(queries, keys, values, starts)


def solution(mesh):
    rows = P(("outer", "inner"), None)
    return jax.shard_map(
        body,
        mesh=mesh,
        in_specs=(rows, rows, rows, P(("outer", "inner"))),
        out_specs=rows,
        check_vma=False,
    )
```

```python
import functools
import math

import jax
import jax.numpy as jnp
from jax import lax
from jax.experimental import pallas as pl
from jax.experimental.pallas import tpu as pltpu
from jax.sharding import PartitionSpec as P

HD = 128
HEADS = 20
TOK = 96
SPAN = 6
COLS = 4
GROUP = HEADS // COLS
ROW = COLS * TOK
BACK = (SPAN - 1) * TOK
KEYS = BACK + ROW
WIN = SPAN * TOK
LAST = 2
MESH = pl.DeviceIdType.MESH
BF16 = jnp.bfloat16


def wrap(a, n):
    return lax.rem(a + n, n)


def device(x, y, z, core):
    return ((y * 4 + lax.rem(z, 4)) * 2 + core, x * 4 + z // 4)


def row_device(x, y, z, core, by, shift):
    r = core * 4 + x + by + 8
    carry = r // 8 - 1
    r = lax.rem(r, 8)
    z2 = wrap(z + shift, 16)
    at = z2 if by > 0 else z
    y2 = wrap(y + carry * ((3 - lax.rem(at, 4)) // 3), 4)
    return device(lax.rem(r, 4), y2, z2, r // 4)


def kernel(q_ref, k_ref, v_ref, start_ref, out_ref, kv, qb, ob, sb, sc, bias,
           kv_send, kv_recv, q_send, q_recv, o_send, o_recv, x_send, x_recv, s_send, s_recv):
    o = lax.axis_index("outer")
    inner = lax.axis_index("inner")
    x, zh = inner // 4, lax.rem(inner, 4)
    core, zl, y = lax.rem(o, 2), lax.rem(o // 2, 4), o // 8
    z = zh * 4 + zl
    r = core * 4 + x

    def ahead(i):
        return (r + i) // 8

    def along(dz):
        return device(x, y, wrap(z + dz, 16), core)

    def column(i):
        return wrap(z - ahead(i), 16) // 4

    def group(i):
        return wrap(column(i) - y, 4)

    barrier = pltpu.get_barrier_semaphore()
    greeted = [along(-4 * n) for n in (1, 2, 3)]
    greeted += [along(-1 - 4 * n) for n in range(4)] + [along(1 + 4 * n - 16) for n in range(4)]
    greeted += [row_device(x, y, z, core, -by, -shift) for by in (1, 2) for shift in (0, 1)]
    for who in greeted:
        pl.semaphore_signal(barrier, inc=1, device_id=who, device_id_type=MESH)

    rows = pl.ds(pl.multiple_of(zh * TOK, TOK), TOK)
    own = pl.ds(pl.multiple_of(BACK + zh * TOK, TOK), TOK)

    def lanes(g, i):
        return pl.ds(pl.multiple_of(g * (GROUP * HD) + i * HD, HD), HD)

    class Copy:
        def __init__(self, src, dst, send, recv, dz, here):
            self.away = pltpu.make_async_remote_copy(
                src_ref=src, dst_ref=dst, send_sem=send, recv_sem=recv,
                device_id=along(dz), device_id_type=MESH)
            self.home = None if here is None else pltpu.make_async_copy(src, dst, recv)
            self.here = here

        def do(self, away, home):
            if self.here is None:
                away(self.away)
                return
            pl.when(self.here == 0)(lambda: home(self.home))
            pl.when(self.here != 0)(lambda: away(self.away))

        def start(self):
            self.do(lambda c: c.start(), lambda c: c.start())

        def wait_recv(self):
            self.do(lambda c: c.wait_recv(), lambda c: c.wait())

        def wait_send(self):
            self.do(lambda c: c.wait_send(), lambda c: None)

    ORDER = (2, 1, 3, 0)

    def kv_copies(i):
        s = ahead(i)
        return [Copy(ref.at[:, lanes(wrap(zh + n - y, 4), i)], kv.at[i, t, own],
                     kv_send.at[t, i, n], kv_recv.at[t, i, n], 4 * n + s, s if n == 0 else None)
                for t, ref in enumerate((k_ref, v_ref)) for n in ORDER]

    def q_copy(i, to):
        s, n = ahead(i), wrap(to - zh, COLS)
        return Copy(q_ref.at[:, lanes(wrap(to - y, COLS), i)], qb.at[i, rows], q_send.at[i, n], q_recv.at[i, n],
                    4 * n + s, n + s)

    def q_here(i, b):
        s, n = ahead(i), wrap(column(i) - b, COLS)
        return Copy(q_ref.at[:, lanes(group(i), i)], qb.at[i, pl.ds(pl.multiple_of(b * TOK, TOK), TOK)],
                    q_send.at[i, n], q_recv.at[i, n], -4 * n - s, n + s)

    def o_copy(i, b):
        s, n = ahead(i), wrap(column(i) - b, COLS)
        return Copy(ob.at[i, pl.ds(pl.multiple_of(b * TOK, TOK), TOK)], out_ref.at[:, lanes(group(i), i)],
                    o_send.at[i, n], o_recv.at[i, n], -4 * n - s, n + s)

    def o_here(i, n):
        s = ahead(i)
        return Copy(ob.at[i, rows], out_ref.at[:, lanes(wrap(zh + n - y, COLS), i)],
                    o_send.at[i, n], o_recv.at[i, n], 4 * n + s, s if n == 0 else None)

    def start_copies():
        return [Copy(start_ref, sb.at[s, zh], s_send.at[s, n], s_recv.at[s, n], 4 * n + s,
                     jnp.int32(0) if n + s == 0 else None) for s in range(2) for n in range(4)]

    def x_copies(i):
        copies = []
        for by, src, dst in ((1, pl.ds(BACK, ROW), pl.ds(TOK, ROW)), (2, pl.ds(KEYS - TOK, TOK), pl.ds(0, TOK))):
            there = r + by
            shift = there // 8 + (lax.rem(there, 8) + i) // 8 - ahead(i)
            copies.append(pltpu.make_async_remote_copy(
                src_ref=kv.at[i, :, src], dst_ref=kv.at[i, :, dst],
                send_sem=x_send.at[by - 1, i], recv_sem=x_recv.at[by - 1, i],
                device_id=row_device(x, y, z, core, by, shift), device_id_type=MESH))
        return copies

    pl.semaphore_wait(barrier, len(greeted))
    for copy in start_copies():
        copy.start()
    for i in range(GROUP):
        for copy in kv_copies(i):
            copy.start()
    for i in range(GROUP - LAST):
        for to in range(COLS):
            q_copy(i, to).start()
    for to in range(COLS):
        for i in range(GROUP - LAST, GROUP):
            q_copy(i, to).start()

    for copy in start_copies():
        copy.wait_recv()
    diagonal = lax.broadcasted_iota(jnp.int32, (TOK, TOK), 0) == lax.broadcasted_iota(jnp.int32, (TOK, TOK), 1)
    for s in range(2):
        for b in range(COLS):
            spread = jnp.broadcast_to(sb[s, b].astype(jnp.float32), (TOK, TOK))
            down = jnp.sum(jnp.where(diagonal, spread, 0.0), axis=1, keepdims=True)
            sc[b * TOK:(b + 1) * TOK, :] = jnp.broadcast_to(down.astype(jnp.int32), (TOK, HD))
        row = ((y * 4 + lax.rem(wrap(z - s, 16), 4)) * 2 + core) * 4 + x
        for b in range(COLS):
            first = row * ROW + b * TOK
            key_pos = first - BACK + lax.broadcasted_iota(jnp.int32, (TOK, WIN), 1)
            query_pos = first + lax.broadcasted_iota(jnp.int32, (TOK, WIN), 0)
            starts = sc[b * TOK:(b + 1) * TOK, 0:1]
            allowed = (key_pos >= starts) & (key_pos <= query_pos)
            bias[s, b] = jnp.where(allowed, 0.0, -jnp.inf)

    @pl.loop(0, GROUP)
    def _(i):
        for copy in kv_copies(i):
            copy.wait_recv()
        for copy in x_copies(i):
            copy.start()

    def block(i, b):
        q_here(i, b).wait_recv()
        low = pl.multiple_of(b * TOK, TOK)
        scores = lax.dot_general(
            qb[i, pl.ds(low, TOK), :], kv[i, 0, pl.ds(low, WIN), :],
            (((1,), (1,)), ((), ())), preferred_element_type=jnp.float32)
        scores = scores * (1.0 / math.sqrt(HD)) + bias[ahead(i), b]
        largest = jnp.max(scores, axis=-1, keepdims=True)
        expsum = jnp.exp(scores - largest)
        total = jnp.sum(expsum, axis=-1, keepdims=True)
        weights = (expsum * (1.0 / total)).astype(BF16)
        mixed = jnp.dot(weights, kv[i, 1, pl.ds(low, WIN), :], preferred_element_type=jnp.float32)
        ob[i, pl.ds(low, TOK), :] = mixed.astype(BF16)
        o_copy(i, b).start()

    @pl.loop(0, GROUP - LAST)
    def _(i):
        for copy in x_copies(i):
            copy.wait_recv()

        @pl.loop(0, COLS)
        def _(b):
            block(i, b)

    for i in range(GROUP - LAST, GROUP):
        for copy in x_copies(i):
            copy.wait_recv()

    @pl.loop(0, COLS)
    def _(b):
        @pl.loop(GROUP - LAST, GROUP)
        def _(i):
            block(i, b)

    for copy in start_copies():
        copy.wait_send()

    @pl.loop(0, GROUP)
    def _(i):
        for copy in kv_copies(i) + x_copies(i):
            copy.wait_send()
        for n in range(COLS):
            o_here(i, n).wait_recv()

        @pl.loop(0, COLS)
        def _(b):
            q_copy(i, b).wait_send()
            o_copy(i, b).wait_send()


def body(queries, keys, values, doc_start):
    starts = doc_start.reshape(1, TOK)
    width = HEADS * HD
    dma = pltpu.SemaphoreType.DMA
    hbm = pl.BlockSpec(memory_space=pltpu.HBM)
    return pl.pallas_call(
        kernel,
        out_shape=jax.ShapeDtypeStruct((TOK, width), jnp.bfloat16),
        in_specs=[hbm, hbm, hbm, hbm],
        out_specs=hbm,
        scratch_shapes=[
            pltpu.VMEM((GROUP, 2, KEYS, HD), jnp.bfloat16),
            pltpu.VMEM((GROUP, ROW, HD), jnp.bfloat16),
            pltpu.VMEM((GROUP, ROW, HD), jnp.bfloat16),
            pltpu.VMEM((2, COLS, 1, TOK), jnp.int32),
            pltpu.VMEM((ROW, HD), jnp.int32),
            pltpu.VMEM((2, COLS, TOK, WIN), jnp.float32),
            dma((2, GROUP, COLS)), dma((2, GROUP, COLS)),
            dma((GROUP, COLS)), dma((GROUP, COLS)),
            dma((GROUP, COLS)), dma((GROUP, COLS)),
            dma((2, GROUP)), dma((2, GROUP)),
            dma((2, COLS)), dma((2, COLS)),
        ],
        compiler_params=pltpu.CompilerParams(
            collective_id=0, has_side_effects=True, vmem_limit_bytes=60 * 1024 * 1024),
        cost_estimate=pl.CostEstimate(
            flops=4 * TOK * SPAN * TOK * width, bytes_accessed=8 * TOK * width,
            transcendentals=TOK * SPAN * TOK * HEADS),
    )(queries, keys, values, starts)


def solution(mesh):
    rows = P(("outer", "inner"), None)
    return jax.shard_map(
        body,
        mesh=mesh,
        in_specs=(rows, rows, rows, P(("outer", "inner"))),
        out_specs=rows,
        check_vma=False,
    )
```

```python
import functools
import math

import jax
import jax.numpy as jnp
from jax import lax
from jax.experimental import pallas as pl
from jax.experimental.pallas import tpu as pltpu
from jax.sharding import PartitionSpec as P

HD = 128
HEADS = 20
TOK = 96
SPAN = 6
COLS = 4
GROUP = HEADS // COLS
ROW = COLS * TOK
BACK = (SPAN - 1) * TOK
KEYS = BACK + ROW
WIN = SPAN * TOK
LAST = 2
MESH = pl.DeviceIdType.MESH
BF16 = jnp.bfloat16


def wrap(a, n):
    return lax.rem(a + n, n)


def device(x, y, z, core):
    return ((y * 4 + lax.rem(z, 4)) * 2 + core, x * 4 + z // 4)


def row_device(x, y, z, core, by, shift):
    r = core * 4 + x + by + 8
    carry = r // 8 - 1
    r = lax.rem(r, 8)
    z2 = wrap(z + shift, 16)
    at = z2 if by > 0 else z
    y2 = wrap(y + carry * ((3 - lax.rem(at, 4)) // 3), 4)
    return device(lax.rem(r, 4), y2, z2, r // 4)


def kernel(q_ref, k_ref, v_ref, start_ref, out_ref, kv, qb, ob, sb, sc, bias,
           kv_send, kv_recv, q_send, q_recv, o_send, o_recv, x_send, x_recv, s_send, s_recv):
    o = lax.axis_index("outer")
    inner = lax.axis_index("inner")
    x, zh = inner // 4, lax.rem(inner, 4)
    core, zl, y = lax.rem(o, 2), lax.rem(o // 2, 4), o // 8
    z = zh * 4 + zl
    r = core * 4 + x

    def ahead(i):
        return (r + i) // 8

    def along(dz):
        return device(x, y, wrap(z + dz, 16), core)

    def column(i):
        return wrap(z - ahead(i), 16) // 4

    def group(i):
        return wrap(column(i) - y, 4)

    barrier = pltpu.get_barrier_semaphore()
    greeted = [along(-4 * n) for n in (1, 2, 3)]
    greeted += [along(-1 - 4 * n) for n in range(4)] + [along(1 + 4 * n - 16) for n in range(4)]
    greeted += [row_device(x, y, z, core, -by, -shift) for by in (1, 2) for shift in (0, 1)]
    for who in greeted:
        pl.semaphore_signal(barrier, inc=1, device_id=who, device_id_type=MESH)

    rows = pl.ds(pl.multiple_of(zh * TOK, TOK), TOK)
    own = pl.ds(pl.multiple_of(BACK + zh * TOK, TOK), TOK)

    def lanes(g, i):
        return pl.ds(pl.multiple_of(g * (GROUP * HD) + i * HD, HD), HD)

    class Copy:
        def __init__(self, src, dst, send, recv, dz, here):
            self.away = pltpu.make_async_remote_copy(
                src_ref=src, dst_ref=dst, send_sem=send, recv_sem=recv,
                device_id=along(dz), device_id_type=MESH)
            self.home = None if here is None else pltpu.make_async_copy(src, dst, recv)
            self.here = here

        def do(self, away, home):
            if self.here is None:
                away(self.away)
                return
            pl.when(self.here == 0)(lambda: home(self.home))
            pl.when(self.here != 0)(lambda: away(self.away))

        def start(self):
            self.do(lambda c: c.start(), lambda c: c.start())

        def wait_recv(self):
            self.do(lambda c: c.wait_recv(), lambda c: c.wait())

        def wait_send(self):
            self.do(lambda c: c.wait_send(), lambda c: None)

    ORDER = (2, 1, 3, 0)

    def kv_copies(i):
        s = ahead(i)
        return [Copy(ref.at[:, lanes(wrap(zh + n - y, 4), i)], kv.at[i, t, own],
                     kv_send.at[t, i, n], kv_recv.at[t, i, n], 4 * n + s, s if n == 0 else None)
                for t, ref in enumerate((k_ref, v_ref)) for n in ORDER]

    def q_copy(i, to):
        s, n = ahead(i), wrap(to - zh, COLS)
        return Copy(q_ref.at[:, lanes(wrap(to - y, COLS), i)], qb.at[i, rows], q_send.at[i, n], q_recv.at[i, n],
                    4 * n + s, n + s)

    def q_here(i, b):
        s, n = ahead(i), wrap(column(i) - b, COLS)
        return Copy(q_ref.at[:, lanes(group(i), i)], qb.at[i, pl.ds(pl.multiple_of(b * TOK, TOK), TOK)],
                    q_send.at[i, n], q_recv.at[i, n], -4 * n - s, n + s)

    def o_copy(i, b):
        s, n = ahead(i), wrap(column(i) - b, COLS)
        return Copy(ob.at[i, pl.ds(pl.multiple_of(b * TOK, TOK), TOK)], out_ref.at[:, lanes(group(i), i)],
                    o_send.at[i, n], o_recv.at[i, n], -4 * n - s, n + s)

    def o_here(i, n):
        s = ahead(i)
        return Copy(ob.at[i, rows], out_ref.at[:, lanes(wrap(zh + n - y, COLS), i)],
                    o_send.at[i, n], o_recv.at[i, n], 4 * n + s, s if n == 0 else None)

    def start_copies():
        return [Copy(start_ref, sb.at[s, zh], s_send.at[s, n], s_recv.at[s, n], 4 * n + s,
                     jnp.int32(0) if n + s == 0 else None) for s in range(2) for n in range(4)]

    def x_copies(i):
        copies = []
        for by, src, dst in ((1, pl.ds(BACK, ROW), pl.ds(TOK, ROW)), (2, pl.ds(KEYS - TOK, TOK), pl.ds(0, TOK))):
            there = r + by
            shift = there // 8 + (lax.rem(there, 8) + i) // 8 - ahead(i)
            copies.append(pltpu.make_async_remote_copy(
                src_ref=kv.at[i, :, src], dst_ref=kv.at[i, :, dst],
                send_sem=x_send.at[by - 1, i], recv_sem=x_recv.at[by - 1, i],
                device_id=row_device(x, y, z, core, by, shift), device_id_type=MESH))
        return copies

    pl.semaphore_wait(barrier, len(greeted))
    for copy in kv_copies(0) + start_copies():
        copy.start()
    for i in range(1, GROUP):
        for copy in kv_copies(i):
            copy.start()

    for copy in start_copies():
        copy.wait_recv()
    diagonal = lax.broadcasted_iota(jnp.int32, (TOK, TOK), 0) == lax.broadcasted_iota(jnp.int32, (TOK, TOK), 1)
    for s in range(2):
        for b in range(COLS):
            spread = jnp.broadcast_to(sb[s, b].astype(jnp.float32), (TOK, TOK))
            down = jnp.sum(jnp.where(diagonal, spread, 0.0), axis=1, keepdims=True)
            sc[b * TOK:(b + 1) * TOK, :] = jnp.broadcast_to(down.astype(jnp.int32), (TOK, HD))
        row = ((y * 4 + lax.rem(wrap(z - s, 16), 4)) * 2 + core) * 4 + x
        for b in range(COLS):
            first = row * ROW + b * TOK
            key_pos = first - BACK + lax.broadcasted_iota(jnp.int32, (TOK, WIN), 1)
            query_pos = first + lax.broadcasted_iota(jnp.int32, (TOK, WIN), 0)
            starts = sc[b * TOK:(b + 1) * TOK, 0:1]
            allowed = (key_pos >= starts) & (key_pos <= query_pos)
            bias[s, b] = jnp.where(allowed, 0.0, -jnp.inf)

    def pass_on(i):
        for copy in kv_copies(i):
            copy.wait_recv()
        for copy in x_copies(i):
            copy.start()

    pass_on(0)
    for i in range(GROUP - LAST):
        for to in range(COLS):
            q_copy(i, to).start()
    for to in range(COLS):
        for i in range(GROUP - LAST, GROUP):
            q_copy(i, to).start()
    pl.loop(1, GROUP)(pass_on)

    def block(i, b):
        q_here(i, b).wait_recv()
        low = pl.multiple_of(b * TOK, TOK)
        scores = lax.dot_general(
            qb[i, pl.ds(low, TOK), :], kv[i, 0, pl.ds(low, WIN), :],
            (((1,), (1,)), ((), ())), preferred_element_type=jnp.float32)
        scores = scores * (1.0 / math.sqrt(HD)) + bias[ahead(i), b]
        largest = jnp.max(scores, axis=-1, keepdims=True)
        expsum = jnp.exp(scores - largest)
        total = jnp.sum(expsum, axis=-1, keepdims=True)
        weights = (expsum * (1.0 / total)).astype(BF16)
        mixed = jnp.dot(weights, kv[i, 1, pl.ds(low, WIN), :], preferred_element_type=jnp.float32)
        ob[i, pl.ds(low, TOK), :] = mixed.astype(BF16)
        o_copy(i, b).start()

    @pl.loop(0, GROUP - LAST)
    def _(i):
        for copy in x_copies(i):
            copy.wait_recv()

        @pl.loop(0, COLS)
        def _(b):
            block(i, b)

    for i in range(GROUP - LAST, GROUP):
        for copy in x_copies(i):
            copy.wait_recv()

    @pl.loop(0, COLS)
    def _(b):
        @pl.loop(GROUP - LAST, GROUP)
        def _(i):
            block(i, b)

    for copy in start_copies():
        copy.wait_send()

    @pl.loop(0, GROUP)
    def _(i):
        for copy in kv_copies(i) + x_copies(i):
            copy.wait_send()
        for n in range(COLS):
            o_here(i, n).wait_recv()

        @pl.loop(0, COLS)
        def _(b):
            q_copy(i, b).wait_send()
            o_copy(i, b).wait_send()


def body(queries, keys, values, doc_start):
    starts = doc_start.reshape(1, TOK)
    width = HEADS * HD
    dma = pltpu.SemaphoreType.DMA
    hbm = pl.BlockSpec(memory_space=pltpu.HBM)
    return pl.pallas_call(
        kernel,
        out_shape=jax.ShapeDtypeStruct((TOK, width), jnp.bfloat16),
        in_specs=[hbm, hbm, hbm, hbm],
        out_specs=hbm,
        scratch_shapes=[
            pltpu.VMEM((GROUP, 2, KEYS, HD), jnp.bfloat16),
            pltpu.VMEM((GROUP, ROW, HD), jnp.bfloat16),
            pltpu.VMEM((GROUP, ROW, HD), jnp.bfloat16),
            pltpu.VMEM((2, COLS, 1, TOK), jnp.int32),
            pltpu.VMEM((ROW, HD), jnp.int32),
            pltpu.VMEM((2, COLS, TOK, WIN), jnp.float32),
            dma((2, GROUP, COLS)), dma((2, GROUP, COLS)),
            dma((GROUP, COLS)), dma((GROUP, COLS)),
            dma((GROUP, COLS)), dma((GROUP, COLS)),
            dma((2, GROUP)), dma((2, GROUP)),
            dma((2, COLS)), dma((2, COLS)),
        ],
        compiler_params=pltpu.CompilerParams(
            collective_id=0, has_side_effects=True, vmem_limit_bytes=60 * 1024 * 1024),
        cost_estimate=pl.CostEstimate(
            flops=4 * TOK * SPAN * TOK * width, bytes_accessed=8 * TOK * width,
            transcendentals=TOK * SPAN * TOK * HEADS),
    )(queries, keys, values, starts)


def solution(mesh):
    rows = P(("outer", "inner"), None)
    return jax.shard_map(
        body,
        mesh=mesh,
        in_specs=(rows, rows, rows, P(("outer", "inner"))),
        out_specs=rows,
        check_vma=False,
    )
```
